32 devices in a mesh: grp: 2 (over x), blk: 16 (over z, y, core).
Axes of the slice: x: 2, y: 2, z: 4, core: 2. Of those that a mesh axis runs over, the one named last changes fastest.
Arguments:
- position: float32 [1536, 64, 128], P(('grp', 'blk')), parts along dimension 0, may hold values from -3 to 3
- momentum: float32 [1536, 64, 128], P(('grp', 'blk')), parts along dimension 0, may hold values from -6 to 6
- counts: int32 [1536, 64, 128], P(('grp', 'blk')), parts along dimension 0, may hold values from 0 to 5
- neighbours: int32 [768, 4], P('blk'), may hold values from -1 to 766, as said below
- cond_factor: bfloat16 [768, 4, 128, 128], P('blk'), may hold values from -0.25 to 0.25
- whiten: bfloat16 [768, 128, 128], P('blk')
Outputs:
- position_end: float32 [1536, 64, 128], P(('grp', 'blk')), parts along dimension 0
- momentum_end: float32 [1536, 64, 128], P(('grp', 'blk')), parts along dimension 0
- energy_change: float32 [128], P('grp'), parts along dimension 0
The draws below stay inside these ranges and needn't reach their ends.
There are 2 independent parts, one for each index of `grp`. The reference program is written for one: setup_inputs(seed, part) draws one part's arguments, and reference() takes and returns one part's arrays. A program takes and returns all parts, laid end to end along the dimension named above; an argument that names none is the same for every part. Nothing has to cross between parts.
Inputs may be any that keep to these rules, and one draw needn't show every extreme that they name: `neighbours`: row b lists block b - 1 first, then three other distinct blocks from b - 96 to b - 2; an entry is -1 exactly where that block would fall before block 0.
All inputs are finite; a program needn't handle non-finite values.
Results may differ from the reference program's by a relative error of at most 0.0018.
Values may be sent and summed in bfloat16 or wider, within the bound.
A program may use at most 128 MiB of HBM per device.

```python
import math
import jax
import jax.numpy as jnp

P_SIZE = 128
C = 64
BLK = 48
NB = 768


def draw_neighbours(key, part):
    key = jax.random.fold_in(key, 5)
    row_keys = jax.random.split(key, NB)
    picks = jax.vmap(lambda one_key: jax.random.permutation(one_key, 2 * BLK - 1)[:3])(row_keys) + 2
    offsets = jnp.concatenate([jnp.ones((NB, 1), jnp.int32), picks.astype(jnp.int32)], axis=1)
    listed = jnp.arange(NB, dtype=jnp.int32)[:, None] - offsets
    return jnp.where(listed < 0, -1, listed).astype(jnp.int32)


def draw_whiten(key, part):
    key = jax.random.fold_in(key, 11)
    noise_key, diag_key = jax.random.split(key)
    noise = jax.random.normal(noise_key, (NB, P_SIZE, P_SIZE), jnp.float32)
    diag_vals = jax.random.uniform(diag_key, (NB, P_SIZE, 1), jnp.float32, 0.8, 1.5)
    rows = jnp.arange(P_SIZE)[:, None]
    cols = jnp.arange(P_SIZE)[None, :]
    lower = jnp.where(cols < rows, noise * (0.5 / math.sqrt(P_SIZE)), 0.0)
    result = lower + jnp.where(rows == cols, diag_vals, 0.0)
    return result.astype(jnp.bfloat16)


def touch_ends(entries, rng, low, high):
    longest = entries.shape.index(max(entries.shape))
    spots = []
    for shift in (0, 1):
        where = [jax.random.randint(jax.random.fold_in(rng, axis), (), 0, length) for axis, length in enumerate(entries.shape)]
        where[longest] = (where[longest] + shift) % entries.shape[longest]
        spots.append(tuple(where))
    return entries.at[spots[0]].set(low).at[spots[1]].set(high)


def steps_of(key, extent, shards, least, largest):
    factor_of, own = 1.0, jax.random.fold_in(key, 6)
    for axis_at, shards_of in shards:
        draws = jnp.exp(jax.random.uniform(jax.random.fold_in(own, axis_at), (shards_of,), jnp.float32, least / len(shards), largest / len(shards)))
        factor_of = factor_of * jnp.repeat(draws, extent[axis_at] // shards_of).reshape([-1 if axis == axis_at else 1 for axis in range(len(extent))])
    return factor_of


def gaussian(own_key, shape, scale, limit, shards=(), kind=jnp.bfloat16):
    values = scale * jax.random.normal(own_key, shape, jnp.float32)
    if shards:
        values = values * steps_of(own_key, shape, shards, -0.22, 0.18)
    return jnp.clip(values, -limit, limit).astype(kind)


def setup_inputs(seed: int = 0, part: int = 0) -> dict:
    keys = jax.random.split(jax.random.key(seed), 7)
    part_splits = jax.random.split(jax.random.fold_in(keys[6], part), 7)
    return {
        "position": gaussian(part_splits[0], (NB, C, P_SIZE), 0.5, 3.0, ((0, 16),), jnp.float32),
        "momentum": gaussian(part_splits[1], (NB, C, P_SIZE), 1.0, 6.0, ((0, 16),), jnp.float32),
        "counts": touch_ends(jax.random.randint(part_splits[2], (NB, C, P_SIZE), 0, 6), jax.random.fold_in(part_splits[2], 1), 0, 5).astype(jnp.int32),
        "neighbours": draw_neighbours(jax.random.fold_in(keys[6], 71), part),
        "cond_factor": gaussian(keys[4], (NB, 4, P_SIZE, P_SIZE), (4 * P_SIZE) ** -0.5, 0.25, ((0, 16),)),
        "whiten": draw_whiten(jax.random.fold_in(keys[6], 71), part),
    }


leap_size = 0.3


def gradient(field, counts, neighbours, cond_factor, whiten):
    present = neighbours >= 0
    safe_index = jnp.where(present, neighbours, 0).astype(jnp.int32)
    rounded = field.astype(jnp.bfloat16)
    nearby = rounded[safe_index] * present.astype(jnp.bfloat16)[:, :, None, None]
    cond_mean = jnp.einsum('bkij,bkcj->bci', cond_factor.astype(jnp.float32), nearby.astype(jnp.float32))
    innovation = (field - cond_mean).astype(jnp.bfloat16)
    whiten_full = whiten.astype(jnp.float32)
    whitened = jnp.einsum('bij,bcj->bci', whiten_full, innovation.astype(jnp.float32))
    pulled = jnp.einsum('bij,bci->bcj', whiten_full, whitened.astype(jnp.bfloat16).astype(jnp.float32))
    pulled_half = pulled.astype(jnp.bfloat16).astype(jnp.float32)
    pushed = -jnp.einsum('bkij,bci->bkcj', cond_factor.astype(jnp.float32), pulled_half)
    pushed = pushed * present.astype(jnp.float32)[:, :, None, None]
    total_blocks = field.shape[0]
    target = jnp.where(present, neighbours, total_blocks).reshape(-1).astype(jnp.int32)
    returned = jax.ops.segment_sum(pushed.reshape((-1,) + field.shape[1:]), target, num_segments=total_blocks + 1)[:total_blocks]
    weight = counts.astype(jnp.float32)
    grad = pulled + returned + jnp.exp(field) - weight
    cell = 0.5 * whitened * whitened + jnp.exp(field) - weight * field
    return grad, cell


def reference(position, momentum, counts, neighbours, cond_factor, whiten):
    grad, cell_start = gradient(position, counts, neighbours, cond_factor, whiten)
    moment = momentum - 0.5 * leap_size * grad
    field = position + leap_size * moment
    grad, cell = gradient(field, counts, neighbours, cond_factor, whiten)
    moment = moment - leap_size * grad
    field = field + leap_size * moment
    grad, cell_end = gradient(field, counts, neighbours, cond_factor, whiten)
    moment = moment - 0.5 * leap_size * grad
    change = cell_end + 0.5 * moment * moment - cell_start - 0.5 * momentum * momentum
    return field, moment, jnp.sum(change, axis=(0, 2))
```

```python
import functools

import jax
import jax.numpy as jnp
from jax import lax
from jax.experimental import pallas as pl
from jax.experimental.pallas import tpu as pltpu
from jax.sharding import PartitionSpec as P

leap_size = 0.3
GROUP = 8


def nt(a, b):
    return lax.dot_general(a, b, (((1,), (1,)), ((), ())), preferred_element_type=jnp.float32)


def nn(a, b):
    return lax.dot_general(a, b, (((1,), (0,)), ((), ())), preferred_element_type=jnp.float32)


def terms_kernel(
    group, slots, far_in, near_in, own_in, field, cond, whiten,
    far_out, near_out, own_out, square_out,
    window, acc, sems,
):
    blocks = far_in.shape[0]
    step = pl.program_id(0)
    steps = pl.num_programs(0)

    @pl.when(step == 0)
    def _():
        copies = [
            pltpu.make_async_copy(part, window.at[pl.ds(at * blocks, blocks)], sems.at[at])
            for at, part in enumerate((far_in, near_in, own_in))
        ]
        for copy in copies:
            copy.start()
        window[3 * blocks] = jnp.zeros(window.shape[1:], window.dtype)
        square_out[...] = jnp.zeros_like(square_out)

        @pl.loop(0, 3 * blocks + 1)
        def _(at):
            acc[at] = jnp.zeros(acc.shape[1:], acc.dtype)

        for copy in copies:
            copy.wait()

    base = step * group
    where = [[slots[(base + g) * 4 + k] for k in range(4)] for g in range(group)]
    innovations = []
    for g in range(group):
        nearby = jnp.concatenate([window[where[g][k]] for k in range(4)], axis=1)
        factor = jnp.concatenate([cond[g, k] for k in range(4)], axis=1)
        innovations.append((field[g] - nt(nearby, factor)).astype(jnp.bfloat16))
    whitened = [nt(innovations[g], whiten[g]) for g in range(group)]
    square = square_out[...]
    for g in range(group):
        square = square + whitened[g] * whitened[g]
    square_out[...] = square
    pulled = [nn(whitened[g].astype(jnp.bfloat16), whiten[g]) for g in range(group)]
    for g in range(group):
        factor = jnp.concatenate([cond[g, k] for k in range(4)], axis=1)
        pushed = nn(pulled[g].astype(jnp.bfloat16), factor)
        points = pulled[g].shape[1]
        for k in range(4):
            acc[where[g][k]] -= pushed[:, k * points : (k + 1) * points]
        acc[2 * blocks + base + g] += pulled[g]

    @pl.when(step == steps - 1)
    def _():
        @pl.loop(0, blocks)
        def _(at):
            far_out[at] = acc[at]
            near_out[at] = acc[blocks + at].astype(near_out.dtype)
            own_out[at] = acc[2 * blocks + at]


def terms(slots, far, near, own, field, cond, whiten):
    blocks, chains, points = field.shape
    group = GROUP if blocks % GROUP == 0 else 1
    whole = pl.BlockSpec((blocks, chains, points), lambda s, i: (0, 0, 0))
    hbm = pl.BlockSpec(memory_space=pl.ANY)
    return pl.pallas_call(
        functools.partial(terms_kernel, group),
        grid_spec=pltpu.PrefetchScalarGridSpec(
            num_scalar_prefetch=1,
            grid=(blocks // group,),
            in_specs=[
                hbm, hbm, hbm,
                pl.BlockSpec((group, chains, points), lambda s, i: (s, 0, 0)),
                pl.BlockSpec((group, 4, points, points), lambda s, i: (s, 0, 0, 0)),
                pl.BlockSpec((group, points, points), lambda s, i: (s, 0, 0)),
            ],
            out_specs=[whole, whole, whole, pl.BlockSpec((chains, points), lambda s, i: (0, 0))],
            scratch_shapes=[
                pltpu.VMEM((3 * blocks + 1, chains, points), jnp.bfloat16),
                pltpu.VMEM((3 * blocks + 1, chains, points), jnp.float32),
                pltpu.SemaphoreType.DMA((3,)),
            ],
        ),
        out_shape=[
            jax.ShapeDtypeStruct(field.shape, jnp.float32),
            jax.ShapeDtypeStruct(field.shape, jnp.bfloat16),
            jax.ShapeDtypeStruct(field.shape, jnp.float32),
            jax.ShapeDtypeStruct((chains, points), jnp.float32),
        ],
        compiler_params=pltpu.CompilerParams(vmem_limit_bytes=40 * 2**20),
        cost_estimate=pl.CostEstimate(
            flops=20 * blocks * chains * points * points, bytes_accessed=20 * 2**20, transcendentals=0
        ),
        name="terms",
    )(slots, far, near, own, field, cond, whiten)


def shifted(value, steps):
    count = lax.axis_size("blk")
    leading, last = (max(0, -steps), min(count, count - steps))
    return lax.ppermute(value, "blk", [(source, source + steps) for source in range(leading, last)])


def swapped(value):
    count = lax.axis_size("blk")
    return lax.ppermute(value, "blk", [(source, source ^ 1) for source in range(count)])


def per_device(position, momentum, counts, neighbours, cond_factor, whiten):
    blocks = position.shape[0]
    me = lax.axis_index("blk")
    odd = lax.rem(me, 2) == 1
    first_block = (me - 2) * blocks
    slots = jnp.where(
        neighbours >= 0, jnp.clip(neighbours - first_block, 0, 3 * blocks - 1), 3 * blocks
    ).reshape(-1)
    weight = counts.astype(jnp.float32)

    def gradient(field):
        rounded = field.astype(jnp.bfloat16)
        farther = shifted(rounded, 2)
        earlier = swapped(jnp.where(odd, farther, rounded))
        far, near, own, square = terms(
            slots, farther, earlier, rounded, field, cond_factor, whiten
        )
        other = swapped(near).astype(jnp.float32)
        back = (far + jnp.where(odd, other, 0.0)).astype(jnp.bfloat16)
        own = own + jnp.where(odd, 0.0, other)
        grad = own + shifted(back, -2).astype(jnp.float32) + jnp.exp(field) - weight
        return grad, square

    def local_cell(field):
        return jnp.exp(field) - weight * field

    grad, square_start = gradient(position)
    moment = momentum - 0.5 * leap_size * grad
    field = position + leap_size * moment
    grad, _ = gradient(field)
    moment = moment - leap_size * grad
    field = field + leap_size * moment
    grad, square_end = gradient(field)
    moment = moment - 0.5 * leap_size * grad
    change = (
        local_cell(field) + 0.5 * moment * moment - local_cell(position) - 0.5 * momentum * momentum
    )
    change = jnp.sum(change, axis=0) + 0.5 * (square_end - square_start)
    total = lax.psum(jnp.sum(change, axis=1), "blk")
    return (field, moment, total)


def solution(mesh):
    return jax.shard_map(
        per_device,
        mesh=mesh,
        in_specs=(
            P(("grp", "blk"), None, None),
            P(("grp", "blk"), None, None),
            P(("grp", "blk"), None, None),
            P("blk", None),
            P("blk", None, None, None),
            P("blk", None, None),
        ),
        out_specs=(P(("grp", "blk"), None, None), P(("grp", "blk"), None, None), P("grp")),
        check_vma=False,
    )
```

```python
import functools

import jax
import jax.numpy as jnp
from jax import lax
from jax.experimental import pallas as pl
from jax.experimental.pallas import tpu as pltpu
from jax.sharding import PartitionSpec as P

leap_size = 0.3
GROUP = 8
PARTS = 6


def nt(a, b):
    return lax.dot_general(a, b, (((1,), (1,)), ((), ())), preferred_element_type=jnp.float32)


def nn(a, b):
    return lax.dot_general(a, b, (((1,), (0,)), ((), ())), preferred_element_type=jnp.float32)


def terms_kernel(
    group, slots, far_in, near_in, own_in, field, cond, whiten,
    far_out, near_out, own_out, square_out,
    window, acc, sems,
):
    blocks = far_in.shape[0]
    step = pl.program_id(0)
    steps = pl.num_programs(0)

    @pl.when(step == 0)
    def _():
        copies = [
            pltpu.make_async_copy(part, window.at[pl.ds(at * blocks, blocks)], sems.at[at])
            for at, part in enumerate((far_in, near_in, own_in))
        ]
        for copy in copies:
            copy.start()
        window[3 * blocks] = jnp.zeros(window.shape[1:], window.dtype)
        square_out[...] = jnp.zeros_like(square_out)

        @pl.loop(0, 3 * blocks + 1)
        def _(at):
            acc[at] = jnp.zeros(acc.shape[1:], acc.dtype)

        for copy in copies:
            copy.wait()

    base = step * group
    where = [[slots[(base + g) * 4 + k] for k in range(4)] for g in range(group)]
    innovations = []
    for g in range(group):
        nearby = jnp.concatenate([window[where[g][k]] for k in range(4)], axis=1)
        factor = jnp.concatenate([cond[g, k] for k in range(4)], axis=1)
        innovations.append((field[g] - nt(nearby, factor)).astype(jnp.bfloat16))
    whitened = [nt(innovations[g], whiten[g]) for g in range(group)]
    square = square_out[...]
    for g in range(group):
        square = square + whitened[g] * whitened[g]
    square_out[...] = square
    pulled = [nn(whitened[g].astype(jnp.bfloat16), whiten[g]) for g in range(group)]
    for g in range(group):
        factor = jnp.concatenate([cond[g, k] for k in range(4)], axis=1)
        pushed = nn(pulled[g].astype(jnp.bfloat16), factor)
        points = pulled[g].shape[1]
        for k in range(4):
            acc[where[g][k]] -= pushed[:, k * points : (k + 1) * points]
        acc[2 * blocks + base + g] += pulled[g]

    @pl.when(step == steps - 1)
    def _():
        @pl.loop(0, blocks)
        def _(at):
            far_out[at] = acc[at]
            near_out[at] = acc[blocks + at].astype(near_out.dtype)
            own_out[at] = acc[2 * blocks + at]


def terms(slots, far, near, own, field, cond, whiten):
    blocks, chains, points = field.shape
    group = GROUP if blocks % GROUP == 0 else 1
    whole = pl.BlockSpec((blocks, chains, points), lambda s, i: (0, 0, 0))
    hbm = pl.BlockSpec(memory_space=pl.ANY)
    return pl.pallas_call(
        functools.partial(terms_kernel, group),
        grid_spec=pltpu.PrefetchScalarGridSpec(
            num_scalar_prefetch=1,
            grid=(blocks // group,),
            in_specs=[
                hbm, hbm, hbm,
                pl.BlockSpec((group, chains, points), lambda s, i: (s, 0, 0)),
                pl.BlockSpec((group, 4, points, points), lambda s, i: (s, 0, 0, 0)),
                pl.BlockSpec((group, points, points), lambda s, i: (s, 0, 0)),
            ],
            out_specs=[whole, whole, whole, pl.BlockSpec((chains, points), lambda s, i: (0, 0))],
            scratch_shapes=[
                pltpu.VMEM((3 * blocks + 1, chains, points), jnp.bfloat16),
                pltpu.VMEM((3 * blocks + 1, chains, points), jnp.float32),
                pltpu.SemaphoreType.DMA((3,)),
            ],
        ),
        out_shape=[
            jax.ShapeDtypeStruct(field.shape, jnp.float32),
            jax.ShapeDtypeStruct(field.shape, jnp.bfloat16),
            jax.ShapeDtypeStruct(field.shape, jnp.float32),
            jax.ShapeDtypeStruct((chains, points), jnp.float32),
        ],
        compiler_params=pltpu.CompilerParams(vmem_limit_bytes=40 * 2**20),
        cost_estimate=pl.CostEstimate(
            flops=20 * blocks * chains * points * points, bytes_accessed=20 * 2**20, transcendentals=0
        ),
        name="terms",
    )(slots, far, near, own, field, cond, whiten)


def exchange_kernel(count, parts, back, forward, coefs, *refs):
    refs = list(refs)
    take = lambda n: [refs.pop(0) for _ in range(n)]
    if back:
        far_hbm, near_hbm, own_hbm, field_hbm, moment_hbm, weight_hbm = take(6)
        field_hbm_out, moment_hbm_out = take(2)
    else:
        (field_hbm,) = take(1)
    if forward:
        far_in, near_in, rounded = take(3)
    if back:
        far, own, field, moment, weight, other, sent, landed = take(8)
        load_sem, store_sem = take(2)
        swap_sem, back_sem = take(2)
    else:
        (field,) = take(1)
        (load_sem,) = take(1)
    if forward:
        pass_sem, pair_sem = take(2)

    me = lax.axis_index("blk")
    odd = lax.rem(me, 2) == 1
    pair = me + 1 - 2 * lax.rem(me, 2)
    has_next = me < count - 2
    has_prev = me >= 2
    blocks = field.shape[0]
    size = blocks // parts
    cut = [pl.ds(c * size, size) for c in range(parts)]

    def load(at, c):
        source, target = loads[at]
        return pltpu.make_async_copy(source.at[cut[c]], target.at[cut[c]], load_sem.at[at, c])

    if back:
        loads = [(far_hbm, far), (own_hbm, own), (field_hbm, field), (moment_hbm, moment), (weight_hbm, weight)]
    else:
        loads = [(field_hbm, field)]
    for at in range(len(loads)):
        for c in range(parts):
            load(at, c).start()

    barrier = pltpu.get_barrier_semaphore()
    pl.semaphore_signal(barrier, inc=1, device_id={"blk": pair}, device_id_type=pl.DeviceIdType.MESH)

    @pl.when(has_next)
    def _():
        pl.semaphore_signal(
            barrier, inc=1, device_id={"blk": me + 2}, device_id_type=pl.DeviceIdType.MESH
        )

    @pl.when(has_prev)
    def _():
        pl.semaphore_signal(
            barrier, inc=1, device_id={"blk": me - 2}, device_id_type=pl.DeviceIdType.MESH
        )

    pl.semaphore_wait(barrier, 1 + has_next.astype(jnp.int32) + has_prev.astype(jnp.int32))

    def remote(source, target, sems, c, device):
        return pltpu.make_async_remote_copy(
            src_ref=source.at[cut[c]], dst_ref=target.at[cut[c]],
            send_sem=sems.at[0, c], recv_sem=sems.at[1, c],
            device_id={"blk": device}, device_id_type=pl.DeviceIdType.MESH,
        )

    swap = lambda c: remote(near_hbm, other, swap_sem, c, pair)
    giving = lambda c: remote(sent, landed, back_sem, c, me - 2)
    passing = lambda c: remote(rounded, far_in, pass_sem, c, me + 2)
    own_to_pair = lambda c: remote(rounded, near_in, pair_sem, c, pair)
    far_to_pair = lambda c: remote(far_in, near_in, pair_sem, c, pair)

    def zero(ref):
        @pl.loop(0, blocks)
        def _(n):
            ref[n] = jnp.zeros(ref.shape[1:], ref.dtype)

    if forward:
        @pl.when(jnp.logical_not(has_prev))
        def _():
            zero(far_in)

    if back:
        for c in range(parts):
            swap(c).start()

        @pl.when(jnp.logical_not(has_next))
        def _():
            zero(landed)

        odd_part = odd.astype(jnp.float32)
        for c in range(parts):
            load(0, c).wait()
            swap(c).wait_recv()

            @pl.loop(c * size, (c + 1) * size)
            def _(n):
                sent[n] = (far[n] + odd_part * other[n].astype(jnp.float32)).astype(sent.dtype)

            @pl.when(has_prev)
            def _():
                giving(c).start()

    for c in range(parts):
        for at in range(1 if back else 0, len(loads)):
            load(at, c).wait()
        if back:
            @pl.when(has_next)
            def _():
                giving(c).wait_recv()

        @pl.loop(c * size, (c + 1) * size)
        def _(n):
            x = field[n]
            if back:
                total = own[n] + (1.0 - odd_part) * other[n].astype(jnp.float32)
                total = total + landed[n].astype(jnp.float32)
                grad = total + jnp.exp(x) - weight[n].astype(jnp.float32)
                m = moment[n] - coefs[0] * grad
                x = x + coefs[1] * m if coefs[1] else x
                moment[n] = m
                if coefs[1]:
                    field[n] = x
            if forward:
                rounded[n] = x.astype(rounded.dtype)

        if forward:
            @pl.when(has_next)
            def _():
                passing(c).start()

            @pl.when(jnp.logical_not(odd))
            def _():
                own_to_pair(c).start()
        if back:
            pltpu.make_async_copy(moment.at[cut[c]], moment_hbm_out.at[cut[c]], store_sem.at[0, c]).start()
            pltpu.make_async_copy(field.at[cut[c]], field_hbm_out.at[cut[c]], store_sem.at[1, c]).start()

    if forward:
        for c in range(parts):
            @pl.when(has_prev)
            def _():
                passing(c).wait_recv()

            @pl.when(odd)
            def _():
                far_to_pair(c).start()

        for c in range(parts):
            own_to_pair(c).wait_recv()
            own_to_pair(c).wait_send()

            @pl.when(has_next)
            def _():
                passing(c).wait_send()

    if back:
        for c in range(parts):
            swap(c).wait_send()

            @pl.when(has_prev)
            def _():
                giving(c).wait_send()

            pltpu.make_async_copy(moment.at[cut[c]], moment_hbm_out.at[cut[c]], store_sem.at[0, c]).wait()
            pltpu.make_async_copy(field.at[cut[c]], field_hbm_out.at[cut[c]], store_sem.at[1, c]).wait()


def exchange(operands, back, forward, coefs, collective_id):
    count = lax.axis_size("blk")
    shape = operands[-1].shape
    blocks = shape[0]
    parts = PARTS if blocks % PARTS == 0 else 1
    hbm = pl.BlockSpec(memory_space=pl.ANY)
    vmem = pl.BlockSpec(memory_space=pltpu.VMEM)
    full, half = jnp.float32, jnp.bfloat16
    out_shape, out_specs, scratch = [], [], []
    if back:
        out_shape += [jax.ShapeDtypeStruct(shape, full)] * 2
        out_specs += [hbm] * 2
    if forward:
        out_shape += [jax.ShapeDtypeStruct(shape, half)] * 3
        out_specs += [vmem] * 3
    sems = lambda n: pltpu.SemaphoreType.DMA((n, parts))
    if back:
        scratch += [pltpu.VMEM(shape, full)] * 4 + [pltpu.VMEM(shape, jnp.int32)]
        scratch += [pltpu.VMEM(shape, half)] * 3
        scratch += [sems(5), sems(2), sems(2), sems(2)]
    else:
        scratch += [pltpu.VMEM(shape, full), sems(1)]
    if forward:
        scratch += [sems(2), sems(2)]
    return pl.pallas_call(
        functools.partial(exchange_kernel, count, parts, back, forward, coefs),
        in_specs=[hbm] * len(operands),
        out_specs=out_specs,
        out_shape=out_shape,
        scratch_shapes=scratch,
        compiler_params=pltpu.CompilerParams(
            vmem_limit_bytes=40 * 2**20, collective_id=collective_id, has_side_effects=True
        ),
        name="exchange",
    )(*operands)


def sum_kernel(count, value, total, slots, send_sem, recv_sem):
    me = lax.axis_index("blk")
    barrier = pltpu.get_barrier_semaphore()

    @pl.loop(1, count)
    def _(d):
        pl.semaphore_signal(
            barrier, inc=1, device_id={"blk": lax.rem(me + d, count)},
            device_id_type=pl.DeviceIdType.MESH,
        )

    pl.semaphore_wait(barrier, count - 1)

    def copy(d):
        return pltpu.make_async_remote_copy(
            src_ref=value, dst_ref=slots.at[d], send_sem=send_sem.at[d], recv_sem=recv_sem.at[d],
            device_id={"blk": lax.rem(me + d, count)}, device_id_type=pl.DeviceIdType.MESH,
        )

    @pl.loop(1, count)
    def _(d):
        copy(d).start()

    total[...] = value[...]

    @pl.loop(1, count)
    def _(d):
        copy(d).wait()
        total[...] += slots[d]


def summed(value, collective_id):
    count = lax.axis_size("blk")
    tile = jnp.zeros((8, 128), jnp.float32).at[0, : value.shape[0]].set(value)
    total = pl.pallas_call(
        functools.partial(sum_kernel, count),
        in_specs=[pl.BlockSpec(memory_space=pltpu.VMEM)],
        out_specs=pl.BlockSpec(memory_space=pltpu.VMEM),
        out_shape=jax.ShapeDtypeStruct(tile.shape, jnp.float32),
        scratch_shapes=[
            pltpu.VMEM((count, 8, 128), jnp.float32),
            pltpu.SemaphoreType.DMA((count,)),
            pltpu.SemaphoreType.DMA((count,)),
        ],
        compiler_params=pltpu.CompilerParams(collective_id=collective_id, has_side_effects=True),
        name="summed",
    )(tile)
    return total[0, : value.shape[0]]


def per_device(position, momentum, counts, neighbours, cond_factor, whiten):
    blocks = position.shape[0]
    first_block = (lax.axis_index("blk") - 2) * blocks
    slots = jnp.where(
        neighbours >= 0, jnp.clip(neighbours - first_block, 0, 3 * blocks - 1), 3 * blocks
    ).reshape(-1)
    weight = counts.astype(jnp.float32)
    h = leap_size

    def pieces(near_by, field):
        return terms(slots, *near_by, field, cond_factor, whiten)

    def local_cell(field):
        return jnp.exp(field) - weight * field

    near_by = exchange((position,), False, True, None, 1)
    far, near, own, square_start = pieces(near_by, position)
    field, moment, *near_by = exchange(
        (far, near, own, position, momentum, counts), True, True, (0.5 * h, h), 2
    )
    far, near, own, _ = pieces(near_by, field)
    field, moment, *near_by = exchange(
        (far, near, own, field, moment, counts), True, True, (h, h), 3
    )
    far, near, own, square_end = pieces(near_by, field)
    _, moment = exchange((far, near, own, field, moment, counts), True, False, (0.5 * h, 0.0), 4)
    change = (
        local_cell(field) + 0.5 * moment * moment - local_cell(position) - 0.5 * momentum * momentum
    )
    change = jnp.sum(change, axis=0) + 0.5 * (square_end - square_start)
    total = summed(jnp.sum(change, axis=1), 5)
    return (field, moment, total)


def solution(mesh):
    return jax.shard_map(
        per_device,
        mesh=mesh,
        in_specs=(
            P(("grp", "blk"), None, None),
            P(("grp", "blk"), None, None),
            P(("grp", "blk"), None, None),
            P("blk", None),
            P("blk", None, None, None),
            P("blk", None, None),
        ),
        out_specs=(P(("grp", "blk"), None, None), P(("grp", "blk"), None, None), P("grp")),
        check_vma=False,
    )
```

```python
import functools

import jax
import jax.numpy as jnp
from jax import lax
from jax.experimental import pallas as pl
from jax.experimental.pallas import tpu as pltpu
from jax.sharding import PartitionSpec as P

leap_size = 0.3
GROUP = 8
PARTS = 6


def nt(a, b):
    return lax.dot_general(a, b, (((1,), (1,)), ((), ())), preferred_element_type=jnp.float32)


def nn(a, b):
    return lax.dot_general(a, b, (((1,), (0,)), ((), ())), preferred_element_type=jnp.float32)


def terms_kernel(
    group, slots, far_in, near_in, own_in, field, cond, whiten,
    far_out, near_out, own_out, square_out, *rest,
):
    window, acc, sems = rest[-3:]
    if len(rest) == 4:
        rest[0][...] = field[...]
    blocks = far_in.shape[0]
    step = pl.program_id(0)
    steps = pl.num_programs(0)

    @pl.when(step == 0)
    def _():
        copies = [
            pltpu.make_async_copy(part, window.at[pl.ds(at * blocks, blocks)], sems.at[at])
            for at, part in enumerate((far_in, near_in, own_in))
        ]
        for copy in copies:
            copy.start()
        window[3 * blocks] = jnp.zeros(window.shape[1:], window.dtype)
        square_out[...] = jnp.zeros_like(square_out)

        @pl.loop(0, 3 * blocks + 1)
        def _(at):
            acc[at] = jnp.zeros(acc.shape[1:], acc.dtype)

        for copy in copies:
            copy.wait()

    base = step * group
    where = [[slots[(base + g) * 4 + k] for k in range(4)] for g in range(group)]
    innovations = []
    for g in range(group):
        nearby = jnp.concatenate([window[where[g][k]] for k in range(4)], axis=1)
        factor = jnp.concatenate([cond[g, k] for k in range(4)], axis=1)
        innovations.append((field[g] - nt(nearby, factor)).astype(jnp.bfloat16))
    whitened = [nt(innovations[g], whiten[g]) for g in range(group)]
    square = square_out[...]
    for g in range(group):
        square = square + whitened[g] * whitened[g]
    square_out[...] = square
    pulled = [nn(whitened[g].astype(jnp.bfloat16), whiten[g]) for g in range(group)]
    for g in range(group):
        factor = jnp.concatenate([cond[g, k] for k in range(4)], axis=1)
        pushed = nn(pulled[g].astype(jnp.bfloat16), factor)
        points = pulled[g].shape[1]
        for k in range(4):
            acc[where[g][k]] -= pushed[:, k * points : (k + 1) * points]
        acc[2 * blocks + base + g] += pulled[g]

    @pl.when(step == steps - 1)
    def _():
        copies = [
            pltpu.make_async_copy(acc.at[pl.ds(0, blocks)], far_out, sems.at[0]),
            pltpu.make_async_copy(acc.at[pl.ds(2 * blocks, blocks)], own_out, sems.at[1]),
        ]
        for copy in copies:
            copy.start()

        @pl.loop(0, blocks)
        def _(at):
            near_out[at] = acc[blocks + at].astype(near_out.dtype)

        for copy in copies:
            copy.wait()


def terms(slots, far, near, own, field, cond, whiten, keep=False):
    blocks, chains, points = field.shape
    group = GROUP if blocks % GROUP == 0 else 1
    whole = pl.BlockSpec((blocks, chains, points), lambda s, i: (0, 0, 0))
    hbm = pl.BlockSpec(memory_space=pl.ANY)
    return pl.pallas_call(
        functools.partial(terms_kernel, group),
        grid_spec=pltpu.PrefetchScalarGridSpec(
            num_scalar_prefetch=1,
            grid=(blocks // group,),
            in_specs=[
                hbm, hbm, hbm,
                pl.BlockSpec((group, chains, points), lambda s, i: (s, 0, 0)),
                pl.BlockSpec((group, 4, points, points), lambda s, i: (s, 0, 0, 0)),
                pl.BlockSpec((group, points, points), lambda s, i: (s, 0, 0)),
            ],
            out_specs=[
                hbm, whole, hbm, pl.BlockSpec((chains, points), lambda s, i: (0, 0)),
                pl.BlockSpec((group, chains, points), lambda s, i: (s, 0, 0)),
            ][: 5 if keep else 4],
            scratch_shapes=[
                pltpu.VMEM((3 * blocks + 1, chains, points), jnp.bfloat16),
                pltpu.VMEM((3 * blocks + 1, chains, points), jnp.float32),
                pltpu.SemaphoreType.DMA((3,)),
            ],
        ),
        out_shape=[
            jax.ShapeDtypeStruct(field.shape, jnp.float32),
            jax.ShapeDtypeStruct(field.shape, jnp.bfloat16),
            jax.ShapeDtypeStruct(field.shape, jnp.float32),
            jax.ShapeDtypeStruct((chains, points), jnp.float32),
            jax.ShapeDtypeStruct(field.shape, jnp.float32),
        ][: 5 if keep else 4],
        compiler_params=pltpu.CompilerParams(vmem_limit_bytes=40 * 2**20),
        cost_estimate=pl.CostEstimate(
            flops=20 * blocks * chains * points * points, bytes_accessed=20 * 2**20, transcendentals=0
        ),
        name="terms",
    )(slots, far, near, own, field, cond, whiten)


def exchange_kernel(count, parts, back, forward, energy, coefs, *refs):
    refs = list(refs)
    take = lambda n: [refs.pop(0) for _ in range(n)]
    if back:
        far_hbm, near_hbm, own_hbm, field_hbm, moment_hbm, weight_hbm = take(6)
        if energy:
            start_hbm, push_hbm, square = take(3)
        moment_hbm_out = take(1)[0]
        if forward:
            field_hbm_out = take(1)[0]
    else:
        (field_hbm,) = take(1)
    if forward:
        forward_out = take(3)
    if energy:
        (total_out,) = take(1)
    if back:
        far, own, field, moment, weight, other, sent, landed = take(8)
        load_sem, store_sem = take(2)
        swap_sem, back_sem = take(2)
    else:
        (field,) = take(1)
        (load_sem,) = take(1)
    if forward:
        far_in, near_in, rounded = take(3)
        pass_sem, pair_sem, out_sem = take(3)
    if energy:
        start, push, gain, slots, sum_send, sum_recv = take(6)

    me = lax.axis_index("blk")
    odd = lax.rem(me, 2) == 1
    pair = me + 1 - 2 * lax.rem(me, 2)
    has_next = me < count - 2
    has_prev = me >= 2
    blocks = field.shape[0]
    size = blocks // parts
    cut = [pl.ds(c * size, size) for c in range(parts)]

    def load(at, c):
        source, target = loads[at]
        return pltpu.make_async_copy(source.at[cut[c]], target.at[cut[c]], load_sem.at[at, c])

    if back:
        loads = [(far_hbm, far), (own_hbm, own), (field_hbm, field), (moment_hbm, moment), (weight_hbm, weight)]
        if energy:
            loads += [(start_hbm, start), (push_hbm, push)]
    else:
        loads = [(field_hbm, field)]
    for at in range(len(loads)):
        for c in range(parts):
            load(at, c).start()

    barrier = pltpu.get_barrier_semaphore()
    pl.semaphore_signal(barrier, inc=1, device_id={"blk": pair}, device_id_type=pl.DeviceIdType.MESH)

    @pl.when(has_next)
    def _():
        pl.semaphore_signal(
            barrier, inc=1, device_id={"blk": me + 2}, device_id_type=pl.DeviceIdType.MESH
        )

    @pl.when(has_prev)
    def _():
        pl.semaphore_signal(
            barrier, inc=1, device_id={"blk": me - 2}, device_id_type=pl.DeviceIdType.MESH
        )

    if energy:
        @pl.loop(1, count)
        def _(d):
            pl.semaphore_signal(
                barrier, inc=1, device_id={"blk": lax.rem(me + d, count)},
                device_id_type=pl.DeviceIdType.MESH,
            )

    pl.semaphore_wait(barrier, (count if energy else 1) + has_next.astype(jnp.int32) + has_prev.astype(jnp.int32))

    def remote(source, target, sems, c, device):
        return pltpu.make_async_remote_copy(
            src_ref=source.at[cut[c]], dst_ref=target.at[cut[c]],
            send_sem=sems.at[0, c], recv_sem=sems.at[1, c],
            device_id={"blk": device}, device_id_type=pl.DeviceIdType.MESH,
        )

    swap = lambda c: remote(near_hbm, other, swap_sem, c, pair)
    giving = lambda c: remote(sent, landed, back_sem, c, me - 2)
    passing = lambda c: remote(rounded, far_in, pass_sem, c, me + 2)
    own_to_pair = lambda c: remote(rounded, near_in, pair_sem, c, pair)
    far_to_pair = lambda c: remote(far_in, near_in, pair_sem, c, pair)

    def keep(at, c):
        return pltpu.make_async_copy(
            (far_in, near_in, rounded)[at].at[cut[c]], forward_out[at].at[cut[c]], out_sem.at[at, c]
        )

    def zero(ref):
        @pl.loop(0, blocks)
        def _(n):
            ref[n] = jnp.zeros(ref.shape[1:], ref.dtype)

    if forward:
        @pl.when(jnp.logical_not(has_prev))
        def _():
            zero(far_in)

    if back:
        for c in range(parts):
            swap(c).start()

        @pl.when(jnp.logical_not(has_next))
        def _():
            zero(landed)

        odd_part = odd.astype(jnp.float32)
        for c in range(parts):
            load(0, c).wait()
            swap(c).wait_recv()

            @pl.loop(c * size, (c + 1) * size)
            def _(n):
                sent[n] = (far[n] + odd_part * other[n].astype(jnp.float32)).astype(sent.dtype)

            @pl.when(has_prev)
            def _():
                giving(c).start()

    if energy:
        gain[...] = 0.5 * square[...]
    for c in range(parts):
        for at in range(1 if back else 0, len(loads)):
            load(at, c).wait()
        if back:
            @pl.when(has_next)
            def _():
                giving(c).wait_recv()

        @pl.loop(c * size, (c + 1) * size)
        def _(n):
            x = field[n]
            if back:
                total = own[n] + (1.0 - odd_part) * other[n].astype(jnp.float32)
                total = total + landed[n].astype(jnp.float32)
                grad = total + jnp.exp(x) - weight[n].astype(jnp.float32)
                m = moment[n] - coefs[0] * grad
                x = x + coefs[1] * m if coefs[1] else x
                moment[n] = m
                if energy:
                    w, x0, m0 = weight[n].astype(jnp.float32), start[n], push[n]
                    gain[...] += (
                        jnp.exp(x) - w * x + 0.5 * m * m
                        - (jnp.exp(x0) - w * x0 + 0.5 * m0 * m0)
                    )
                if coefs[1]:
                    field[n] = x
            if forward:
                rounded[n] = x.astype(rounded.dtype)

        if forward:
            keep(2, c).start()

            @pl.when(has_next)
            def _():
                passing(c).start()

            @pl.when(jnp.logical_not(odd))
            def _():
                own_to_pair(c).start()
        if back:
            pltpu.make_async_copy(moment.at[cut[c]], moment_hbm_out.at[cut[c]], store_sem.at[0, c]).start()
            if forward:
                pltpu.make_async_copy(field.at[cut[c]], field_hbm_out.at[cut[c]], store_sem.at[1, c]).start()

    if forward:
        for c in range(parts):
            @pl.when(has_prev)
            def _():
                passing(c).wait_recv()

            @pl.when(odd)
            def _():
                far_to_pair(c).start()

            keep(0, c).start()

        for c in range(parts):
            own_to_pair(c).wait_recv()
            keep(1, c).start()

        for c in range(parts):
            for at in range(3):
                keep(at, c).wait()
            own_to_pair(c).wait_send()

            @pl.when(has_next)
            def _():
                passing(c).wait_send()

    if energy:
        def spread(d):
            return pltpu.make_async_remote_copy(
                src_ref=slots.at[0], dst_ref=slots.at[d],
                send_sem=sum_send.at[d], recv_sem=sum_recv.at[d],
                device_id={"blk": lax.rem(me + d, count)}, device_id_type=pl.DeviceIdType.MESH,
            )

        chains, points = gain.shape
        lanes = slots.shape[2]
        column = jnp.broadcast_to(jnp.sum(gain[...], axis=1, keepdims=True), (chains, lanes))
        row = lax.broadcasted_iota(jnp.int32, (chains, lanes), 0)
        lane = lax.broadcasted_iota(jnp.int32, (chains, lanes), 1)
        line = jnp.sum(jnp.where(row == lane, column, 0.0), axis=0, keepdims=True)
        slots[0] = jnp.broadcast_to(line, slots.shape[1:])

        @pl.loop(1, count)
        def _(d):
            spread(d).start()

        total_out[...] = slots[0]

        @pl.loop(1, count)
        def _(d):
            spread(d).wait()
            total_out[...] += slots[d]

    if back:
        for c in range(parts):
            swap(c).wait_send()

            @pl.when(has_prev)
            def _():
                giving(c).wait_send()

            pltpu.make_async_copy(moment.at[cut[c]], moment_hbm_out.at[cut[c]], store_sem.at[0, c]).wait()
            if forward:
                pltpu.make_async_copy(field.at[cut[c]], field_hbm_out.at[cut[c]], store_sem.at[1, c]).wait()


def exchange(operands, back, forward, coefs, collective_id, energy=False):
    count = lax.axis_size("blk")
    shape = operands[5 if back else 0].shape
    lanes = -(-shape[1] // 128) * 128
    blocks = shape[0]
    parts = PARTS if blocks % PARTS == 0 else 1
    hbm = pl.BlockSpec(memory_space=pl.ANY)
    vmem = pl.BlockSpec(memory_space=pltpu.VMEM)
    full, half = jnp.float32, jnp.bfloat16
    out_shape, out_specs, scratch = [], [], []
    if back:
        out_shape += [jax.ShapeDtypeStruct(shape, full)] * (2 if forward else 1)
        out_specs += [hbm] * (2 if forward else 1)
    if forward:
        out_shape += [jax.ShapeDtypeStruct(shape, half)] * 3
        out_specs += [hbm] * 3
    if energy:
        out_shape += [jax.ShapeDtypeStruct((8, lanes), full)]
        out_specs += [vmem]
    sems = lambda n: pltpu.SemaphoreType.DMA((n, parts))
    if back:
        scratch += [pltpu.VMEM(shape, full)] * 4 + [pltpu.VMEM(shape, jnp.int32)]
        scratch += [pltpu.VMEM(shape, half)] * 3
        scratch += [sems(7 if energy else 5), sems(2), sems(2), sems(2)]
    else:
        scratch += [pltpu.VMEM(shape, full), sems(1)]
    if forward:
        scratch += [pltpu.VMEM(shape, half)] * 3 + [sems(2), sems(2), sems(3)]
    if energy:
        scratch += [
            pltpu.VMEM(shape, full), pltpu.VMEM(shape, full), pltpu.VMEM(shape[1:], full),
            pltpu.VMEM((count, 8, lanes), full),
            pltpu.SemaphoreType.DMA((count,)), pltpu.SemaphoreType.DMA((count,)),
        ]
    return pl.pallas_call(
        functools.partial(exchange_kernel, count, parts, back, forward, energy, coefs),
        in_specs=[hbm] * 8 + [vmem] if energy else [hbm] * len(operands),
        out_specs=out_specs,
        out_shape=out_shape,
        scratch_shapes=scratch,
        compiler_params=pltpu.CompilerParams(
            vmem_limit_bytes=40 * 2**20, collective_id=collective_id, has_side_effects=True
        ),
        name="exchange",
    )(*operands)


def per_device(position, momentum, counts, neighbours, cond_factor, whiten):
    blocks = position.shape[0]
    first_block = (lax.axis_index("blk") - 2) * blocks
    slots = jnp.where(
        neighbours >= 0, jnp.clip(neighbours - first_block, 0, 3 * blocks - 1), 3 * blocks
    ).reshape(-1)
    h = leap_size

    def pieces(near_by, field, keep=False):
        return terms(slots, *near_by, field, cond_factor, whiten, keep)

    near_by = exchange((position,), False, True, None, 1)
    far, near, own, square_start = pieces(near_by, position)
    moment, field, *near_by = exchange(
        (far, near, own, position, momentum, counts), True, True, (0.5 * h, h), 2
    )
    far, near, own, _ = pieces(near_by, field)
    moment, field, *near_by = exchange(
        (far, near, own, field, moment, counts), True, True, (h, h), 3
    )
    far, near, own, square_end, field_end = pieces(near_by, field, True)
    moment, total = exchange(
        (far, near, own, field, moment, counts, position, momentum, square_end - square_start),
        True, False, (0.5 * h, 0.0), 4, True,
    )
    return (field_end, moment, total[0, : position.shape[1]])


def solution(mesh):
    return jax.shard_map(
        per_device,
        mesh=mesh,
        in_specs=(
            P(("grp", "blk"), None, None),
            P(("grp", "blk"), None, None),
            P(("grp", "blk"), None, None),
            P("blk", None),
            P("blk", None, None, None),
            P("blk", None, None),
        ),
        out_specs=(P(("grp", "blk"), None, None), P(("grp", "blk"), None, None), P("grp")),
        check_vma=False,
    )
```

```python
import functools

import jax
import jax.numpy as jnp
from jax import lax
from jax.experimental import pallas as pl
from jax.experimental.pallas import tpu as pltpu
from jax.sharding import PartitionSpec as P

leap_size = 0.3
GROUP = 16
PARTS = 6


def nt(a, b):
    return lax.dot_general(a, b, (((1,), (1,)), ((), ())), preferred_element_type=jnp.float32)


def nn(a, b):
    return lax.dot_general(a, b, (((1,), (0,)), ((), ())), preferred_element_type=jnp.float32)


def terms_kernel(
    group, slots, far_in, near_in, own_in, field, cond, whiten,
    far_out, near_out, own_out, square_out, *rest,
):
    window, acc, sems = rest[-3:]
    if len(rest) == 4:
        rest[0][...] = field[...]
    blocks = far_in.shape[0]
    step = pl.program_id(0)
    steps = pl.num_programs(0)

    @pl.when(step == 0)
    def _():
        copies = [
            pltpu.make_async_copy(part, window.at[pl.ds(at * blocks, blocks)], sems.at[at])
            for at, part in enumerate((far_in, near_in, own_in))
        ]
        for copy in copies:
            copy.start()
        window[3 * blocks] = jnp.zeros(window.shape[1:], window.dtype)
        square_out[...] = jnp.zeros_like(square_out)

        @pl.loop(0, 3 * blocks + 1)
        def _(at):
            acc[at] = jnp.zeros(acc.shape[1:], acc.dtype)

        for copy in copies:
            copy.wait()

    base = step * group
    where = [[slots[(base + g) * 4 + k] for k in range(4)] for g in range(group)]
    innovations = []
    for g in range(group):
        nearby = jnp.concatenate([window[where[g][k]] for k in range(4)], axis=1)
        factor = jnp.concatenate([cond[g, k] for k in range(4)], axis=1)
        innovations.append((field[g] - nt(nearby, factor)).astype(jnp.bfloat16))
    whitened = [nt(innovations[g], whiten[g]) for g in range(group)]
    square = square_out[...]
    for g in range(group):
        square = square + whitened[g] * whitened[g]
    square_out[...] = square
    pulled = [nn(whitened[g].astype(jnp.bfloat16), whiten[g]) for g in range(group)]
    for g in range(group):
        factor = jnp.concatenate([cond[g, k] for k in range(4)], axis=1)
        pushed = nn(pulled[g].astype(jnp.bfloat16), factor)
        points = pulled[g].shape[1]
        for k in range(4):
            acc[where[g][k]] -= pushed[:, k * points : (k + 1) * points]
        acc[2 * blocks + base + g] += pulled[g]

    @pl.when(step == steps - 1)
    def _():
        copies = [
            pltpu.make_async_copy(acc.at[pl.ds(0, blocks)], far_out, sems.at[0]),
            pltpu.make_async_copy(acc.at[pl.ds(2 * blocks, blocks)], own_out, sems.at[1]),
        ]
        for copy in copies:
            copy.start()

        @pl.loop(0, blocks)
        def _(at):
            near_out[at] = acc[blocks + at].astype(near_out.dtype)

        for copy in copies:
            copy.wait()


def terms(slots, far, near, own, field, cond, whiten, keep=False):
    blocks, chains, points = field.shape
    group = GROUP if blocks % GROUP == 0 else 1
    whole = pl.BlockSpec((blocks, chains, points), lambda s, i: (0, 0, 0))
    hbm = pl.BlockSpec(memory_space=pl.ANY)
    return pl.pallas_call(
        functools.partial(terms_kernel, group),
        grid_spec=pltpu.PrefetchScalarGridSpec(
            num_scalar_prefetch=1,
            grid=(blocks // group,),
            in_specs=[
                hbm, hbm, hbm,
                pl.BlockSpec((group, chains, points), lambda s, i: (s, 0, 0)),
                pl.BlockSpec((group, 4, points, points), lambda s, i: (s, 0, 0, 0)),
                pl.BlockSpec((group, points, points), lambda s, i: (s, 0, 0)),
            ],
            out_specs=[
                hbm, whole, hbm, pl.BlockSpec((chains, points), lambda s, i: (0, 0)),
                pl.BlockSpec((group, chains, points), lambda s, i: (s, 0, 0)),
            ][: 5 if keep else 4],
            scratch_shapes=[
                pltpu.VMEM((3 * blocks + 1, chains, points), jnp.bfloat16),
                pltpu.VMEM((3 * blocks + 1, chains, points), jnp.float32),
                pltpu.SemaphoreType.DMA((3,)),
            ],
        ),
        out_shape=[
            jax.ShapeDtypeStruct(field.shape, jnp.float32),
            jax.ShapeDtypeStruct(field.shape, jnp.bfloat16),
            jax.ShapeDtypeStruct(field.shape, jnp.float32),
            jax.ShapeDtypeStruct((chains, points), jnp.float32),
            jax.ShapeDtypeStruct(field.shape, jnp.float32),
        ][: 5 if keep else 4],
        compiler_params=pltpu.CompilerParams(vmem_limit_bytes=40 * 2**20),
        cost_estimate=pl.CostEstimate(
            flops=20 * blocks * chains * points * points, bytes_accessed=20 * 2**20, transcendentals=0
        ),
        name="terms",
    )(slots, far, near, own, field, cond, whiten)


def exchange_kernel(count, parts, back, forward, energy, coefs, *refs):
    refs = list(refs)
    take = lambda n: [refs.pop(0) for _ in range(n)]
    if back:
        far_hbm, near_hbm, own_hbm, field_hbm, moment_hbm, weight_hbm = take(6)
        if energy:
            start_hbm, push_hbm, square = take(3)
        moment_hbm_out = take(1)[0]
        if forward:
            field_hbm_out = take(1)[0]
    else:
        (field_hbm,) = take(1)
    if forward:
        forward_out = take(3)
    if energy:
        (total_out,) = take(1)
    if back:
        far, own, field, moment, weight, other, sent, landed = take(8)
        load_sem, store_sem = take(2)
        swap_sem, back_sem = take(2)
    else:
        (field,) = take(1)
        (load_sem,) = take(1)
    if forward:
        far_in, near_in, rounded = take(3)
        pass_sem, pair_sem, out_sem = take(3)
    if energy:
        start, push, gain, slots, sum_send, sum_recv = take(6)

    me = lax.axis_index("blk")
    odd = lax.rem(me, 2) == 1
    pair = me + 1 - 2 * lax.rem(me, 2)
    has_next = me < count - 2
    has_prev = me >= 2
    blocks = field.shape[0]
    size = blocks // parts
    cut = [pl.ds(c * size, size) for c in range(parts)]

    def load(at, c):
        source, target = loads[at]
        return pltpu.make_async_copy(source.at[cut[c]], target.at[cut[c]], load_sem.at[at, c])

    if back:
        loads = [(far_hbm, far), (own_hbm, own), (field_hbm, field), (moment_hbm, moment), (weight_hbm, weight)]
        if energy:
            loads += [(start_hbm, start), (push_hbm, push)]
    else:
        loads = [(field_hbm, field)]
    for at in range(len(loads)):
        for c in range(parts):
            load(at, c).start()

    barrier = pltpu.get_barrier_semaphore()
    pl.semaphore_signal(barrier, inc=1, device_id={"blk": pair}, device_id_type=pl.DeviceIdType.MESH)

    @pl.when(has_next)
    def _():
        pl.semaphore_signal(
            barrier, inc=1, device_id={"blk": me + 2}, device_id_type=pl.DeviceIdType.MESH
        )

    @pl.when(has_prev)
    def _():
        pl.semaphore_signal(
            barrier, inc=1, device_id={"blk": me - 2}, device_id_type=pl.DeviceIdType.MESH
        )

    if energy:
        @pl.loop(1, count)
        def _(d):
            pl.semaphore_signal(
                barrier, inc=1, device_id={"blk": lax.rem(me + d, count)},
                device_id_type=pl.DeviceIdType.MESH,
            )

    pl.semaphore_wait(barrier, (count if energy else 1) + has_next.astype(jnp.int32) + has_prev.astype(jnp.int32))

    def remote(source, target, sems, c, device):
        return pltpu.make_async_remote_copy(
            src_ref=source.at[cut[c]], dst_ref=target.at[cut[c]],
            send_sem=sems.at[0, c], recv_sem=sems.at[1, c],
            device_id={"blk": device}, device_id_type=pl.DeviceIdType.MESH,
        )

    swap = lambda c: remote(near_hbm, other, swap_sem, c, pair)
    giving = lambda c: remote(sent, landed, back_sem, c, me - 2)
    passing = lambda c: remote(rounded, far_in, pass_sem, c, me + 2)
    own_to_pair = lambda c: remote(rounded, near_in, pair_sem, c, pair)
    far_to_pair = lambda c: remote(far_in, near_in, pair_sem, c, pair)

    def keep(at, c):
        return pltpu.make_async_copy(
            (far_in, near_in, rounded)[at].at[cut[c]], forward_out[at].at[cut[c]], out_sem.at[at, c]
        )

    def zero(ref):
        @pl.loop(0, blocks)
        def _(n):
            ref[n] = jnp.zeros(ref.shape[1:], ref.dtype)

    if forward:
        @pl.when(jnp.logical_not(has_prev))
        def _():
            zero(far_in)

    if back:
        for c in range(parts):
            swap(c).start()

        @pl.when(jnp.logical_not(has_next))
        def _():
            zero(landed)

        odd_part = odd.astype(jnp.float32)
        for c in range(parts):
            load(0, c).wait()
            swap(c).wait_recv()

            @pl.loop(c * size, (c + 1) * size)
            def _(n):
                sent[n] = (far[n] + odd_part * other[n].astype(jnp.float32)).astype(sent.dtype)

            @pl.when(has_prev)
            def _():
                giving(c).start()

    if energy:
        gain[...] = 0.5 * square[...]
    for c in range(parts):
        for at in range(1 if back else 0, len(loads)):
            load(at, c).wait()
        if back:
            @pl.when(has_next)
            def _():
                giving(c).wait_recv()

        @pl.loop(c * size, (c + 1) * size)
        def _(n):
            x = field[n]
            if back:
                total = own[n] + (1.0 - odd_part) * other[n].astype(jnp.float32)
                total = total + landed[n].astype(jnp.float32)
                grad = total + jnp.exp(x) - weight[n].astype(jnp.float32)
                m = moment[n] - coefs[0] * grad
                x = x + coefs[1] * m if coefs[1] else x
                moment[n] = m
                if energy:
                    w, x0, m0 = weight[n].astype(jnp.float32), start[n], push[n]
                    gain[...] += (
                        jnp.exp(x) - w * x + 0.5 * m * m
                        - (jnp.exp(x0) - w * x0 + 0.5 * m0 * m0)
                    )
                if coefs[1]:
                    field[n] = x
            if forward:
                rounded[n] = x.astype(rounded.dtype)

        if forward:
            keep(2, c).start()

            @pl.when(has_next)
            def _():
                passing(c).start()

            @pl.when(jnp.logical_not(odd))
            def _():
                own_to_pair(c).start()
        if back:
            pltpu.make_async_copy(moment.at[cut[c]], moment_hbm_out.at[cut[c]], store_sem.at[0, c]).start()
            if forward:
                pltpu.make_async_copy(field.at[cut[c]], field_hbm_out.at[cut[c]], store_sem.at[1, c]).start()

    if forward:
        for c in range(parts):
            @pl.when(has_prev)
            def _():
                passing(c).wait_recv()

            @pl.when(odd)
            def _():
                far_to_pair(c).start()

            keep(0, c).start()

        for c in range(parts):
            own_to_pair(c).wait_recv()
            keep(1, c).start()

        for c in range(parts):
            for at in range(3):
                keep(at, c).wait()
            own_to_pair(c).wait_send()

            @pl.when(has_next)
            def _():
                passing(c).wait_send()

    if energy:
        def spread(d):
            return pltpu.make_async_remote_copy(
                src_ref=slots.at[0], dst_ref=slots.at[d],
                send_sem=sum_send.at[d], recv_sem=sum_recv.at[d],
                device_id={"blk": lax.rem(me + d, count)}, device_id_type=pl.DeviceIdType.MESH,
            )

        chains, points = gain.shape
        lanes = slots.shape[2]
        column = jnp.broadcast_to(jnp.sum(gain[...], axis=1, keepdims=True), (chains, lanes))
        row = lax.broadcasted_iota(jnp.int32, (chains, lanes), 0)
        lane = lax.broadcasted_iota(jnp.int32, (chains, lanes), 1)
        line = jnp.sum(jnp.where(row == lane, column, 0.0), axis=0, keepdims=True)
        slots[0] = jnp.broadcast_to(line, slots.shape[1:])

        @pl.loop(1, count)
        def _(d):
            spread(d).start()

        total_out[...] = slots[0]

        @pl.loop(1, count)
        def _(d):
            spread(d).wait()
            total_out[...] += slots[d]

    if back:
        for c in range(parts):
            swap(c).wait_send()

            @pl.when(has_prev)
            def _():
                giving(c).wait_send()

            pltpu.make_async_copy(moment.at[cut[c]], moment_hbm_out.at[cut[c]], store_sem.at[0, c]).wait()
            if forward:
                pltpu.make_async_copy(field.at[cut[c]], field_hbm_out.at[cut[c]], store_sem.at[1, c]).wait()


def exchange(operands, back, forward, coefs, collective_id, energy=False):
    count = lax.axis_size("blk")
    shape = operands[5 if back else 0].shape
    lanes = -(-shape[1] // 128) * 128
    blocks = shape[0]
    parts = PARTS if blocks % PARTS == 0 else 1
    hbm = pl.BlockSpec(memory_space=pl.ANY)
    vmem = pl.BlockSpec(memory_space=pltpu.VMEM)
    full, half = jnp.float32, jnp.bfloat16
    out_shape, out_specs, scratch = [], [], []
    if back:
        out_shape += [jax.ShapeDtypeStruct(shape, full)] * (2 if forward else 1)
        out_specs += [hbm] * (2 if forward else 1)
    if forward:
        out_shape += [jax.ShapeDtypeStruct(shape, half)] * 3
        out_specs += [hbm] * 3
    if energy:
        out_shape += [jax.ShapeDtypeStruct((8, lanes), full)]
        out_specs += [vmem]
    sems = lambda n: pltpu.SemaphoreType.DMA((n, parts))
    if back:
        scratch += [pltpu.VMEM(shape, full)] * 4 + [pltpu.VMEM(shape, jnp.int32)]
        scratch += [pltpu.VMEM(shape, half)] * 3
        scratch += [sems(7 if energy else 5), sems(2), sems(2), sems(2)]
    else:
        scratch += [pltpu.VMEM(shape, full), sems(1)]
    if forward:
        scratch += [pltpu.VMEM(shape, half)] * 3 + [sems(2), sems(2), sems(3)]
    if energy:
        scratch += [
            pltpu.VMEM(shape, full), pltpu.VMEM(shape, full), pltpu.VMEM(shape[1:], full),
            pltpu.VMEM((count, 8, lanes), full),
            pltpu.SemaphoreType.DMA((count,)), pltpu.SemaphoreType.DMA((count,)),
        ]
    return pl.pallas_call(
        functools.partial(exchange_kernel, count, parts, back, forward, energy, coefs),
        in_specs=[hbm] * 8 + [vmem] if energy else [hbm] * len(operands),
        out_specs=out_specs,
        out_shape=out_shape,
        scratch_shapes=scratch,
        compiler_params=pltpu.CompilerParams(
            vmem_limit_bytes=40 * 2**20, collective_id=collective_id, has_side_effects=True
        ),
        name="exchange",
    )(*operands)


def per_device(position, momentum, counts, neighbours, cond_factor, whiten):
    blocks = position.shape[0]
    first_block = (lax.axis_index("blk") - 2) * blocks
    slots = jnp.where(
        neighbours >= 0, jnp.clip(neighbours - first_block, 0, 3 * blocks - 1), 3 * blocks
    ).reshape(-1)
    h = leap_size

    def pieces(near_by, field, keep=False):
        return terms(slots, *near_by, field, cond_factor, whiten, keep)

    near_by = exchange((position,), False, True, None, 1)
    far, near, own, square_start = pieces(near_by, position)
    moment, field, *near_by = exchange(
        (far, near, own, position, momentum, counts), True, True, (0.5 * h, h), 2
    )
    far, near, own, _ = pieces(near_by, field)
    moment, field, *near_by = exchange(
        (far, near, own, field, moment, counts), True, True, (h, h), 3
    )
    far, near, own, square_end, field_end = pieces(near_by, field, True)
    moment, total = exchange(
        (far, near, own, field, moment, counts, position, momentum, square_end - square_start),
        True, False, (0.5 * h, 0.0), 4, True,
    )
    return (field_end, moment, total[0, : position.shape[1]])


def solution(mesh):
    return jax.shard_map(
        per_device,
        mesh=mesh,
        in_specs=(
            P(("grp", "blk"), None, None),
            P(("grp", "blk"), None, None),
            P(("grp", "blk"), None, None),
            P("blk", None),
            P("blk", None, None, None),
            P("blk", None, None),
        ),
        out_specs=(P(("grp", "blk"), None, None), P(("grp", "blk"), None, None), P("grp")),
        check_vma=False,
    )
```

```python
import functools

import jax
import jax.numpy as jnp
from jax import lax
from jax.experimental import pallas as pl
from jax.experimental.pallas import tpu as pltpu
from jax.sharding import PartitionSpec as P

leap_size = 0.3
GROUP = 16
PARTS = 6


def nt(a, b):
    return lax.dot_general(a, b, (((1,), (1,)), ((), ())), preferred_element_type=jnp.float32)


def nn(a, b):
    return lax.dot_general(a, b, (((1,), (0,)), ((), ())), preferred_element_type=jnp.float32)


def terms_kernel(
    group, slots, far_in, near_in, own_in, field, cond, whiten,
    far_out, near_out, own_out, square_out, *rest,
):
    window, acc, sems = rest[-3:]
    if len(rest) == 4:
        rest[0][...] = field[...]
    blocks = far_in.shape[0]
    step = pl.program_id(0)
    steps = pl.num_programs(0)

    @pl.when(step == 0)
    def _():
        copies = [
            pltpu.make_async_copy(part, window.at[pl.ds(at * blocks, blocks)], sems.at[at])
            for at, part in enumerate((far_in, near_in, own_in))
        ]
        for copy in copies:
            copy.start()
        window[3 * blocks] = jnp.zeros(window.shape[1:], window.dtype)
        square_out[...] = jnp.zeros_like(square_out)

        @pl.loop(0, 3 * blocks + 1)
        def _(at):
            acc[at] = jnp.zeros(acc.shape[1:], acc.dtype)

        for copy in copies:
            copy.wait()

    base = step * group
    where = [[slots[(base + g) * 4 + k] for k in range(4)] for g in range(group)]
    innovations = []
    for g in range(group):
        nearby = jnp.concatenate([window[where[g][k]] for k in range(4)], axis=1)
        factor = jnp.concatenate([cond[g, k] for k in range(4)], axis=1)
        innovations.append((field[g] - nt(nearby, factor)).astype(jnp.bfloat16))
    whitened = [nt(innovations[g], whiten[g]) for g in range(group)]
    square = square_out[...]
    for g in range(group):
        square = square + whitened[g] * whitened[g]
    square_out[...] = square
    pulled = [nn(whitened[g].astype(jnp.bfloat16), whiten[g]) for g in range(group)]
    for g in range(group):
        factor = jnp.concatenate([cond[g, k] for k in range(4)], axis=1)
        pushed = nn(pulled[g].astype(jnp.bfloat16), factor)
        points = pulled[g].shape[1]
        for k in range(4):
            acc[where[g][k]] -= pushed[:, k * points : (k + 1) * points]
        acc[2 * blocks + base + g] += pulled[g]

    @pl.when(step == steps - 1)
    def _():
        copies = [
            pltpu.make_async_copy(acc.at[pl.ds(0, blocks)], far_out, sems.at[0]),
            pltpu.make_async_copy(acc.at[pl.ds(2 * blocks, blocks)], own_out, sems.at[1]),
        ]
        for copy in copies:
            copy.start()

        @pl.loop(0, blocks)
        def _(at):
            near_out[at] = acc[blocks + at].astype(near_out.dtype)

        for copy in copies:
            copy.wait()


def terms(slots, far, near, own, field, cond, whiten, keep=False):
    blocks, chains, points = field.shape
    group = GROUP if blocks % GROUP == 0 else 1
    whole = pl.BlockSpec((blocks, chains, points), lambda s, i: (0, 0, 0))
    hbm = pl.BlockSpec(memory_space=pl.ANY)
    return pl.pallas_call(
        functools.partial(terms_kernel, group),
        grid_spec=pltpu.PrefetchScalarGridSpec(
            num_scalar_prefetch=1,
            grid=(blocks // group,),
            in_specs=[
                hbm, hbm, hbm,
                pl.BlockSpec((group, chains, points), lambda s, i: (s, 0, 0)),
                pl.BlockSpec((group, 4, points, points), lambda s, i: (s, 0, 0, 0)),
                pl.BlockSpec((group, points, points), lambda s, i: (s, 0, 0)),
            ],
            out_specs=[
                hbm, whole, hbm, pl.BlockSpec((chains, points), lambda s, i: (0, 0)),
                pl.BlockSpec((group, chains, points), lambda s, i: (s, 0, 0)),
            ][: 5 if keep else 4],
            scratch_shapes=[
                pltpu.VMEM((3 * blocks + 1, chains, points), jnp.bfloat16),
                pltpu.VMEM((3 * blocks + 1, chains, points), jnp.float32),
                pltpu.SemaphoreType.DMA((3,)),
            ],
        ),
        out_shape=[
            jax.ShapeDtypeStruct(field.shape, jnp.float32),
            jax.ShapeDtypeStruct(field.shape, jnp.bfloat16),
            jax.ShapeDtypeStruct(field.shape, jnp.float32),
            jax.ShapeDtypeStruct((chains, points), jnp.float32),
            jax.ShapeDtypeStruct(field.shape, jnp.float32),
        ][: 5 if keep else 4],
        compiler_params=pltpu.CompilerParams(vmem_limit_bytes=40 * 2**20),
        cost_estimate=pl.CostEstimate(
            flops=20 * blocks * chains * points * points, bytes_accessed=20 * 2**20, transcendentals=0
        ),
        name="terms",
    )(slots, far, near, own, field, cond, whiten)


def exchange_kernel(count, parts, back, forward, energy, coefs, *refs):
    refs = list(refs)
    take = lambda n: [refs.pop(0) for _ in range(n)]
    if back:
        far_hbm, near_hbm, own_hbm, field_hbm, moment_hbm, weight_hbm = take(6)
        if energy:
            start_hbm, push_hbm, square = take(3)
        moment_hbm_out = take(1)[0]
        if forward:
            field_hbm_out = take(1)[0]
    else:
        (field_hbm,) = take(1)
    if forward:
        forward_out = take(3)
    if energy:
        (total_out,) = take(1)
    if back:
        far, own, field, moment, weight, other, sent, landed = take(8)
        load_sem, store_sem = take(2)
        swap_sem, back_sem = take(2)
    else:
        (field,) = take(1)
        (load_sem,) = take(1)
    if forward:
        far_in, near_in, rounded = take(3)
        pass_sem, pair_sem, out_sem = take(3)
    if energy:
        start, push, gain, slots, sum_send, sum_recv = take(6)

    me = lax.axis_index("blk")
    odd = lax.rem(me, 2) == 1
    pair = me + 1 - 2 * lax.rem(me, 2)
    has_next = me < count - 2
    has_prev = me >= 2
    blocks = field.shape[0]
    size = blocks // parts
    cut = [pl.ds(c * size, size) for c in range(parts)]

    def load(at, c):
        source, target = loads[at]
        if at:
            return pltpu.make_async_copy(source, target, load_sem.at[at, 0])
        return pltpu.make_async_copy(source.at[cut[c]], target.at[cut[c]], load_sem.at[at, c])

    if back:
        loads = [(far_hbm, far), (own_hbm, own), (field_hbm, field), (moment_hbm, moment), (weight_hbm, weight)]
        if energy:
            loads += [(start_hbm, start), (push_hbm, push)]
    else:
        loads = [(field_hbm, field)]
    for c in range(parts):
        load(0, c).start()

    barrier = pltpu.get_barrier_semaphore()
    pl.semaphore_signal(barrier, inc=1, device_id={"blk": pair}, device_id_type=pl.DeviceIdType.MESH)

    @pl.when(has_next)
    def _():
        pl.semaphore_signal(
            barrier, inc=1, device_id={"blk": me + 2}, device_id_type=pl.DeviceIdType.MESH
        )

    @pl.when(has_prev)
    def _():
        pl.semaphore_signal(
            barrier, inc=1, device_id={"blk": me - 2}, device_id_type=pl.DeviceIdType.MESH
        )

    if energy:
        @pl.loop(1, count)
        def _(d):
            pl.semaphore_signal(
                barrier, inc=1, device_id={"blk": lax.rem(me + d, count)},
                device_id_type=pl.DeviceIdType.MESH,
            )

    pl.semaphore_wait(barrier, (count if energy else 1) + has_next.astype(jnp.int32) + has_prev.astype(jnp.int32))

    def remote(source, target, sems, c, device):
        return pltpu.make_async_remote_copy(
            src_ref=source.at[cut[c]], dst_ref=target.at[cut[c]],
            send_sem=sems.at[0, c], recv_sem=sems.at[1, c],
            device_id={"blk": device}, device_id_type=pl.DeviceIdType.MESH,
        )

    swap = lambda c: remote(near_hbm, other, swap_sem, c, pair)
    giving = lambda c: remote(sent, landed, back_sem, c, me - 2)
    passing = lambda c: remote(rounded, far_in, pass_sem, c, me + 2)
    own_to_pair = lambda c: remote(rounded, near_in, pair_sem, c, pair)
    far_to_pair = lambda c: remote(far_in, near_in, pair_sem, c, pair)

    def keep(at, c):
        return pltpu.make_async_copy(
            (far_in, near_in, rounded)[at].at[cut[c]], forward_out[at].at[cut[c]], out_sem.at[at, c]
        )

    def zero(ref):
        @pl.loop(0, blocks)
        def _(n):
            ref[n] = jnp.zeros(ref.shape[1:], ref.dtype)

    if forward:
        @pl.when(jnp.logical_not(has_prev))
        def _():
            zero(far_in)

    if back:
        for c in range(parts):
            swap(c).start()
        for at in range(1, len(loads)):
            load(at, 0).start()

        @pl.when(jnp.logical_not(has_next))
        def _():
            zero(landed)

        odd_part = odd.astype(jnp.float32)
        for c in range(parts):
            load(0, c).wait()
            swap(c).wait_recv()

            @pl.loop(c * size, (c + 1) * size)
            def _(n):
                sent[n] = (far[n] + odd_part * other[n].astype(jnp.float32)).astype(sent.dtype)

            @pl.when(has_prev)
            def _():
                giving(c).start()

    if energy:
        gain[...] = 0.5 * square[...]
    for c in range(parts):
        if not back:
            load(0, c).wait()
        elif c == 0:
            for at in range(1, len(loads)):
                load(at, 0).wait()
        if back:
            @pl.when(has_next)
            def _():
                giving(c).wait_recv()

        @pl.loop(c * size, (c + 1) * size)
        def _(n):
            x = field[n]
            if back:
                total = own[n] + (1.0 - odd_part) * other[n].astype(jnp.float32)
                total = total + landed[n].astype(jnp.float32)
                grad = total + jnp.exp(x) - weight[n].astype(jnp.float32)
                m = moment[n] - coefs[0] * grad
                x = x + coefs[1] * m if coefs[1] else x
                moment[n] = m
                if energy:
                    w, x0, m0 = weight[n].astype(jnp.float32), start[n], push[n]
                    gain[...] += (
                        jnp.exp(x) - w * x + 0.5 * m * m
                        - (jnp.exp(x0) - w * x0 + 0.5 * m0 * m0)
                    )
                if coefs[1]:
                    field[n] = x
            if forward:
                rounded[n] = x.astype(rounded.dtype)

        if forward:
            keep(2, c).start()

            @pl.when(has_next)
            def _():
                passing(c).start()

            @pl.when(jnp.logical_not(odd))
            def _():
                own_to_pair(c).start()
        if back:
            pltpu.make_async_copy(moment.at[cut[c]], moment_hbm_out.at[cut[c]], store_sem.at[0, c]).start()
            if forward:
                pltpu.make_async_copy(field.at[cut[c]], field_hbm_out.at[cut[c]], store_sem.at[1, c]).start()

    if forward:
        for c in range(parts):
            @pl.when(has_prev)
            def _():
                passing(c).wait_recv()

            @pl.when(odd)
            def _():
                far_to_pair(c).start()

            keep(0, c).start()

        for c in range(parts):
            own_to_pair(c).wait_recv()
            keep(1, c).start()

        for c in range(parts):
            for at in range(3):
                keep(at, c).wait()
            own_to_pair(c).wait_send()

            @pl.when(has_next)
            def _():
                passing(c).wait_send()

    if energy:
        def spread(d):
            return pltpu.make_async_remote_copy(
                src_ref=slots.at[0], dst_ref=slots.at[d],
                send_sem=sum_send.at[d], recv_sem=sum_recv.at[d],
                device_id={"blk": lax.rem(me + d, count)}, device_id_type=pl.DeviceIdType.MESH,
            )

        chains, points = gain.shape
        lanes = slots.shape[2]
        column = jnp.broadcast_to(jnp.sum(gain[...], axis=1, keepdims=True), (chains, lanes))
        row = lax.broadcasted_iota(jnp.int32, (chains, lanes), 0)
        lane = lax.broadcasted_iota(jnp.int32, (chains, lanes), 1)
        line = jnp.sum(jnp.where(row == lane, column, 0.0), axis=0, keepdims=True)
        slots[0] = jnp.broadcast_to(line, slots.shape[1:])

        @pl.loop(1, count)
        def _(d):
            spread(d).start()

        total_out[...] = slots[0]

        @pl.loop(1, count)
        def _(d):
            spread(d).wait()
            total_out[...] += slots[d]

    if back:
        for c in range(parts):
            swap(c).wait_send()

            @pl.when(has_prev)
            def _():
                giving(c).wait_send()

            pltpu.make_async_copy(moment.at[cut[c]], moment_hbm_out.at[cut[c]], store_sem.at[0, c]).wait()
            if forward:
                pltpu.make_async_copy(field.at[cut[c]], field_hbm_out.at[cut[c]], store_sem.at[1, c]).wait()


def exchange(operands, back, forward, coefs, collective_id, energy=False):
    count = lax.axis_size("blk")
    shape = operands[5 if back else 0].shape
    lanes = -(-shape[1] // 128) * 128
    blocks = shape[0]
    parts = PARTS if blocks % PARTS == 0 else 1
    hbm = pl.BlockSpec(memory_space=pl.ANY)
    vmem = pl.BlockSpec(memory_space=pltpu.VMEM)
    full, half = jnp.float32, jnp.bfloat16
    out_shape, out_specs, scratch = [], [], []
    if back:
        out_shape += [jax.ShapeDtypeStruct(shape, full)] * (2 if forward else 1)
        out_specs += [hbm] * (2 if forward else 1)
    if forward:
        out_shape += [jax.ShapeDtypeStruct(shape, half)] * 3
        out_specs += [hbm] * 3
    if energy:
        out_shape += [jax.ShapeDtypeStruct((8, lanes), full)]
        out_specs += [vmem]
    sems = lambda n: pltpu.SemaphoreType.DMA((n, parts))
    if back:
        scratch += [pltpu.VMEM(shape, full)] * 4 + [pltpu.VMEM(shape, jnp.int32)]
        scratch += [pltpu.VMEM(shape, half)] * 3
        scratch += [sems(7 if energy else 5), sems(2), sems(2), sems(2)]
    else:
        scratch += [pltpu.VMEM(shape, full), sems(1)]
    if forward:
        scratch += [pltpu.VMEM(shape, half)] * 3 + [sems(2), sems(2), sems(3)]
    if energy:
        scratch += [
            pltpu.VMEM(shape, full), pltpu.VMEM(shape, full), pltpu.VMEM(shape[1:], full),
            pltpu.VMEM((count, 8, lanes), full),
            pltpu.SemaphoreType.DMA((count,)), pltpu.SemaphoreType.DMA((count,)),
        ]
    return pl.pallas_call(
        functools.partial(exchange_kernel, count, parts, back, forward, energy, coefs),
        in_specs=[hbm] * 8 + [vmem] if energy else [hbm] * len(operands),
        out_specs=out_specs,
        out_shape=out_shape,
        scratch_shapes=scratch,
        compiler_params=pltpu.CompilerParams(
            vmem_limit_bytes=40 * 2**20, collective_id=collective_id, has_side_effects=True
        ),
        name="exchange",
    )(*operands)


def per_device(position, momentum, counts, neighbours, cond_factor, whiten):
    blocks = position.shape[0]
    first_block = (lax.axis_index("blk") - 2) * blocks
    slots = jnp.where(
        neighbours >= 0, jnp.clip(neighbours - first_block, 0, 3 * blocks - 1), 3 * blocks
    ).reshape(-1)
    h = leap_size

    def pieces(near_by, field, keep=False):
        return terms(slots, *near_by, field, cond_factor, whiten, keep)

    near_by = exchange((position,), False, True, None, 1)
    far, near, own, square_start = pieces(near_by, position)
    moment, field, *near_by = exchange(
        (far, near, own, position, momentum, counts), True, True, (0.5 * h, h), 2
    )
    far, near, own, _ = pieces(near_by, field)
    moment, field, *near_by = exchange(
        (far, near, own, field, moment, counts), True, True, (h, h), 3
    )
    far, near, own, square_end, field_end = pieces(near_by, field, True)
    moment, total = exchange(
        (far, near, own, field, moment, counts, position, momentum, square_end - square_start),
        True, False, (0.5 * h, 0.0), 4, True,
    )
    return (field_end, moment, total[0, : position.shape[1]])


def solution(mesh):
    return jax.shard_map(
        per_device,
        mesh=mesh,
        in_specs=(
            P(("grp", "blk"), None, None),
            P(("grp", "blk"), None, None),
            P(("grp", "blk"), None, None),
            P("blk", None),
            P("blk", None, None, None),
            P("blk", None, None),
        ),
        out_specs=(P(("grp", "blk"), None, None), P(("grp", "blk"), None, None), P("grp")),
        check_vma=False,
    )
```
